256 devices in a mesh: rep: 32 (over z_hi, y, x), node: 8 (over z_lo, core).
Axes of the slice: x: 4, y: 4, z: 8 (z_hi: 2, z_lo: 4; z = z_hi * 4 + z_lo), core: 2. Of those that a mesh axis runs over, the one named last changes fastest.
Arguments:
- attention: bfloat16 [65536, 2048], P(('rep', 'node')), may hold values from -6 to 6
- cotangent: bfloat16 [65536, 1792], P(('rep', 'node')), may hold values from -6 to 6
- token_ids: int32 [65536], P(('rep', 'node')), may hold values from 0 to 255999, as said below
- out_weight: bfloat16 [32, 2048, 1792], P('rep', 'node'), may hold values from -0.125 to 0.125
- moment: float32 [32, 2048, 1792], P('rep', 'node'), may hold values from -60 to 60
- second: float32 [32, 2048, 1792], P('rep', 'node'), may hold values from 100 to 4000
- norm_gain: float32 [32, 1792], P('rep'), may hold values from -0.5 to 0.5
- frag_index: int32 [1], replicated, may hold values from 0 to 7
- outer_delta: float32 [32, 8, 131072], P('rep', 'node'), may hold values from -6 to 6
- anchors: float32 [8, 131072], P(None, 'node'), may hold values from -6 to 6
- momenta: float32 [8, 131072], P(None, 'node'), may hold values from -3 to 3
- local_fragment: float32 [32, 131072], P('rep', 'node'), may hold values from -6 to 6
Outputs:
- new_weight: bfloat16 [32, 2048, 1792], P('rep', 'node')
- new_moment: float32 [32, 2048, 1792], P('rep', 'node')
- new_second: float32 [32, 2048, 1792], P('rep', 'node')
- grad_attention: bfloat16 [65536, 2048], P(('rep', 'node'))
- new_anchors: float32 [8, 131072], P(None, 'node')
- new_momenta: float32 [8, 131072], P(None, 'node')
- merged: float32 [32, 131072], P('rep')
The draws below stay inside these ranges and needn't reach their ends.
Inputs may be any that keep to these rules, and one draw needn't show every extreme that they name: `token_ids`: 0 marks padding; every other entry is a vocabulary id.
All inputs are finite; a program needn't handle non-finite values.
Results may differ from the reference program's by a relative error of at most 0.015.
Values may be sent and summed in bfloat16 or wider, within the bound.
No kernel may reach another device: no remote copies, remote signals or barrier semaphores. Data moves between devices by JAX's collectives and lax.ppermute only.
A program may use at most 128 MiB of HBM per device.

```python
import math
import jax
import jax.numpy as jnp
from jax import lax

D = 1792
VOCAB = 256000
TOK_DEV = 256
FRAGS = 8
H = 2048
TOKENS = 65536
FRAG = 131072
N_REP = 32
N_NODE = 8


def draw_token_ids(key, part):
    key = jax.random.fold_in(key, 11)
    first_key, second_key = jax.random.split(key)
    drawn = jax.random.randint(first_key, (TOKENS,), 1, VOCAB)
    padding = jax.random.randint(second_key, (TOKENS,), 0, 4)
    result = jnp.where(padding == 0, 0, drawn)
    result = result.at[0].set(VOCAB - 1)
    result = result.at[1].set(0)
    return result.astype(jnp.int32)


def raised(values, own_key, source, target, parts, factor):
    owner, partner = [(jnp.arange(values.shape[dim]) // (values.shape[dim] // parts)).reshape([-1 if axis == dim else 1 for axis in range(values.ndim)]) for dim in (source, target)]
    chosen = jax.random.permutation(own_key, parts)[partner]
    strong = (owner == chosen) | (owner == (partner + parts // 2) % parts)
    return jnp.where(strong, factor * values, values)


def level_of(rng, shape, cuts, least, top_value):
    def one(axis_at, blocks):
        draws = jax.random.uniform(jax.random.fold_in(jax.random.fold_in(rng, 6), axis_at), (blocks,), jnp.float32, least / len(cuts), top_value / len(cuts))
        return jnp.repeat(jnp.exp(draws), shape[axis_at] // blocks).reshape((-1,) + (1,) * (len(shape) - axis_at - 1))

    loudness = one(*cuts[0])
    for cut in cuts[1:]:
        loudness = loudness * one(*cut)
    return loudness


def gaussian(rng, dims, deviation, bound, cuts=(), held_as=jnp.bfloat16):
    entries = jax.random.normal(rng, dims, jnp.float32) * deviation
    if len(cuts) > 0:
        entries = level_of(rng, dims, cuts, -0.22, 0.18) * entries
    return jnp.clip(entries, min=-bound, max=bound).astype(held_as)


def gaussian_with(stream_key, dims, spread, reach, cuts, heavy, kind=jnp.bfloat16):
    values = spread * jax.random.normal(stream_key, dims, jnp.float32)
    if cuts:
        values = values * level_of(stream_key, dims, cuts, -0.22, 0.18)
    return jnp.clip(raised(values, jax.random.fold_in(stream_key, 3), *heavy), -reach, reach).astype(kind)


def setup_inputs(seed: int = 0) -> dict:
    key_of = jax.random.split(jax.random.key(seed), 13)
    return {
        "attention": gaussian(key_of[0], (TOKENS, H), 1.0, 6.0, ((0, 256),)),
        "cotangent": gaussian(key_of[1], (TOKENS, D), 1.0, 6.0, ((0, 256),)),
        "token_ids": draw_token_ids(jax.random.fold_in(key_of[12], 71), 0),
        "out_weight": gaussian(key_of[3], (N_REP, H, D), H ** -0.5, 0.125, ((0, 32), (1, 8))),
        "moment": gaussian(key_of[4], (N_REP, H, D), 10.0, 60.0, ((0, 32), (1, 8)), jnp.float32),
        "second": jnp.clip(jnp.exp(math.log(4000.0) - 3.6888795 * jax.random.uniform(key_of[5], (N_REP, H, D), jnp.float32) ** level_of(key_of[5], (N_REP, H, D), ((0, 32), (1, 8)), -0.2, 0.2)), 100.0, 4000.0),
        "norm_gain": jnp.clip(jax.random.uniform(key_of[6], (N_REP, D), jnp.float32, -0.5, 0.5) * level_of(key_of[6], (N_REP, D), ((0, 32),), -0.4, 0.0), -0.5, 0.5),
        "frag_index": jax.random.randint(key_of[7], (1,), 0, FRAGS).astype(jnp.int32),
        "outer_delta": gaussian_with(key_of[8], (N_REP, N_NODE, FRAG), 1.0, 6.0, ((0, 32), (1, 8)), (0, 2, 32, 2.75), jnp.float32),
        "anchors": gaussian(key_of[9], (FRAGS, FRAG), 1.0, 6.0, ((1, 8),), jnp.float32),
        "momenta": gaussian(key_of[10], (FRAGS, FRAG), 0.5, 3.0, ((1, 8),), jnp.float32),
        "local_fragment": gaussian(key_of[11], (N_REP, FRAG), 1.0, 6.0, ((0, 32), (1, 8)), jnp.float32),
    }


beta_one = 0.9
beta_two = 0.95
adam_eps = 1e-08
inner_rate = 0.001
decay_rate = 0.1
inner_step = 10.0
outer_momentum = 0.9
outer_rate = 0.7
merge_weight = 0.5

def post_norm(values, gain):
    meansq = lax.optimization_barrier(jnp.mean(values * values, axis=-1, keepdims=True))
    return values * lax.rsqrt(meansq + 1e-06) * (1.0 + gain)

def adamw(weight, moment, second, gradient):
    moment_new = beta_one * moment + (1.0 - beta_one) * gradient
    second_new = beta_two * second + (1.0 - beta_two) * gradient * gradient
    moment_hat = moment_new / (1.0 - beta_one ** inner_step)
    second_hat = second_new / (1.0 - beta_two ** inner_step)
    master = weight.astype(jnp.float32)
    updated = master - inner_rate * (moment_hat / (jnp.sqrt(second_hat) + adam_eps) + decay_rate * master)
    return (updated.astype(jnp.bfloat16), moment_new, second_new)

def replica_step(operands):
    attention, cotangent, token_ids, weight, moment, second, gain = operands
    projected = jnp.dot(attention, weight, preferred_element_type=jnp.float32)
    loss_mask = (token_ids != 0).astype(jnp.float32)
    weighted = cotangent.astype(jnp.float32) * loss_mask[:, None]
    _, pullback = jax.vjp(lambda values: post_norm(values, gain), projected)
    dprojected = pullback(weighted)[0].astype(jnp.bfloat16)
    gradient = jnp.dot(attention.T, dprojected, preferred_element_type=jnp.float32)
    grad_attention = jnp.dot(dprojected, weight.T, preferred_element_type=jnp.float32).astype(jnp.bfloat16)
    new_weight, new_moment, new_second = adamw(weight, moment, second, gradient)
    return (new_weight, new_moment, new_second, grad_attention)

def reference(attention, cotangent, token_ids, out_weight, moment, second, norm_gain, frag_index, outer_delta, anchors, momenta, local_fragment):
    rows = N_NODE * TOK_DEV
    operands = (attention.reshape(N_REP, rows, H), cotangent.reshape(N_REP, rows, D), token_ids.reshape(N_REP, rows), out_weight, moment, second, norm_gain)
    new_weight, new_moment, new_second, grad_attention = lax.map(replica_step, operands)
    grad_attention = grad_attention.reshape(N_REP * rows, H)
    summed = lax.optimization_barrier(jnp.sum(outer_delta, axis=(0, 1)))
    average = summed / N_REP
    index = frag_index[0].astype(jnp.int32)
    anchor = lax.dynamic_index_in_dim(anchors, index, 0, keepdims=False)
    previous = lax.dynamic_index_in_dim(momenta, index, 0, keepdims=False)
    momentum = outer_momentum * previous + average
    anchor_new = anchor - outer_rate * (average + outer_momentum * momentum)
    new_anchors = lax.dynamic_update_index_in_dim(anchors, anchor_new, index, 0)
    new_momenta = lax.dynamic_update_index_in_dim(momenta, momentum, index, 0)
    merged = merge_weight * local_fragment + (1.0 - merge_weight) * anchor_new[None, :]
    return (new_weight, new_moment, new_second, grad_attention, new_anchors, new_momenta, merged)
```

```python
import jax
import jax.numpy as jnp
from jax import lax
from jax.sharding import PartitionSpec as P

beta_one = 0.9
beta_two = 0.95
adam_eps = 1e-08
inner_rate = 0.001
decay_rate = 0.1
inner_step = 10.0
outer_momentum = 0.9
outer_rate = 0.7
merge_weight = 0.5

NODES = 8
CHIPS = 4
CHUNKS = 2

RING = [(a, (a + 2) % NODES) for a in range(NODES)]


def adamw(weight, moment, second, gradient):
    moment_new = beta_one * moment + (1.0 - beta_one) * gradient
    second_new = beta_two * second + (1.0 - beta_two) * gradient * gradient
    moment_hat = moment_new / (1.0 - beta_one**inner_step)
    second_hat = second_new / (1.0 - beta_two**inner_step)
    master = weight.astype(jnp.float32)
    updated = master - inner_rate * (
        moment_hat / (jnp.sqrt(second_hat) + adam_eps) + decay_rate * master
    )
    return (updated.astype(jnp.bfloat16), moment_new, second_new)


def nesterov(average, anchor, previous):
    momentum = outer_momentum * previous + average
    anchor_new = anchor - outer_rate * (average + outer_momentum * momentum)
    return (anchor_new, momentum)


def after(value, *others):
    return lax.optimization_barrier((value, *others))[0]


def swapped(value, axis, size, mask):
    return lax.ppermute(value, axis, [(a, a ^ mask) for a in range(size)])


def on_device(
    attention,
    cotangent,
    token_ids,
    out_weight,
    moment,
    second,
    norm_gain,
    frag_index,
    outer_delta,
    anchors,
    momenta,
    local_fragment,
):
    node = lax.axis_index("node")
    replicas = lax.axis_size("rep")
    chip, core = node // 2, node % 2
    weight_shard = out_weight[0]
    gain = 1.0 + norm_gain[0]
    rows, width = weight_shard.shape
    tokens, features = attention.shape
    part = rows // CHUNKS
    span = width // CHUNKS
    f32 = jnp.float32

    def turn(step):
        return (chip - step) % CHIPS

    ring = [[weight_shard[h * part : (h + 1) * part] for h in range(CHUNKS)]]
    twin = [[swapped(piece, "node", NODES, 1) for piece in ring[0]]]
    for _ in range(CHIPS - 1):
        ring.append([lax.ppermute(piece, "node", RING) for piece in ring[-1]])
        twin.append([swapped(piece, "node", NODES, 1) for piece in ring[-1]])

    def columns(owner):
        return lax.dynamic_slice(attention, (0, owner * rows), (tokens, rows))

    own_cols = [columns(turn(step) * 2 + core) for step in range(CHIPS)]
    twin_cols = [columns(turn(step) * 2 + 1 - core) for step in range(CHIPS)]
    lent = swapped(jnp.stack(twin_cols), "node", NODES, 1)
    own_t = [jnp.transpose(block) for block in own_cols]
    lent_t = [jnp.transpose(lent[step]) for step in range(CHIPS)]

    projected = jnp.zeros((tokens, width), f32)
    for step in range(CHIPS):
        for h in range(CHUNKS):
            at = slice(h * part, (h + 1) * part)
            projected += jnp.dot(
                own_cols[step][:, at], ring[step][h], preferred_element_type=f32
            )
            projected += jnp.dot(
                twin_cols[step][:, at], twin[step][h], preferred_element_type=f32
            )

    loss_mask = (token_ids != 0).astype(f32)
    meansq = jnp.mean(projected * projected, axis=-1, keepdims=True)
    scale = lax.rsqrt(meansq + 1e-06)
    weighted = cotangent.astype(f32) * loss_mask[:, None] * gain
    inner = jnp.mean(weighted * projected, axis=-1, keepdims=True)
    dprojected = (scale * weighted - (scale * scale * scale * inner) * projected).astype(
        jnp.bfloat16
    )
    dtwin = swapped(dprojected, "node", NODES, 1)

    def partial(step, h):
        at = slice(h * span, (h + 1) * span)
        step %= CHIPS
        return jnp.dot(own_t[step], dprojected[:, at], preferred_element_type=f32) + jnp.dot(
            lent_t[step], dtwin[:, at], preferred_element_type=f32
        )

    travelling = [partial(1, h).astype(jnp.bfloat16) for h in range(CHUNKS)]
    back = []
    for step in range(2, CHIPS + 1):
        arrived = [lax.ppermute(piece, "node", RING) for piece in travelling]
        back.append(arrived)
        sums = [arrived[h].astype(f32) + partial(step, h) for h in range(CHUNKS)]
        travelling = [piece.astype(jnp.bfloat16) for piece in sums]
    gradient = jnp.concatenate(sums, axis=1)
    new_weight, new_moment, new_second = adamw(weight_shard, moment[0], second[0], gradient)

    grad_attention = jnp.zeros((tokens, features), jnp.bfloat16)
    contract = (((1,), (1,)), ((), ()))
    held_back = after(dprojected, back[0][0])
    for step in range(CHIPS):
        for at, held in ((core, ring), (1 - core, twin)):
            block = lax.dot_general(
                held_back,
                jnp.concatenate(held[step], axis=0),
                contract,
                preferred_element_type=f32,
            ).astype(jnp.bfloat16)
            grad_attention = lax.dynamic_update_slice(
                grad_attention, block, (0, (turn(step) * 2 + at) * rows)
            )

    parts = outer_delta[0, 0].reshape(CHIPS, 2, -1)
    give = lax.dynamic_index_in_dim(parts, 1 - core, 1, keepdims=False)
    keep = lax.dynamic_index_in_dim(parts, core, 1, keepdims=False)
    got = swapped(give.astype(jnp.bfloat16), "node", NODES, 1)
    shards = keep + after(got, ring[1][0]).astype(f32)

    def for_chip(other):
        return lax.dynamic_index_in_dim(shards, other, 0, keepdims=False)

    got = [
        swapped(for_chip(chip ^ m).astype(jnp.bfloat16), "node", NODES, 2 * m)
        for m in range(1, CHIPS)
    ]
    got = after(jnp.stack(got), ring[1][1]).astype(f32)
    total = (for_chip(chip) + got[0]) + (got[1] + got[2])
    for unit, late in ((1, ring[2][0]), (4, ring[2][1])):
        got = [swapped(total, "rep", replicas, m * unit) for m in range(1, 4)]
        got = after(jnp.stack(got), late)
        total = (total + got[0]) + (got[1] + got[2])
    rounded = total.astype(jnp.bfloat16)
    got = swapped(rounded, "rep", replicas, 16)
    summed = rounded.astype(f32) + after(got, ring[3][0]).astype(f32)

    index = frag_index[0]
    anchor = lax.dynamic_index_in_dim(anchors, index, 0, keepdims=False)
    previous = lax.dynamic_index_in_dim(momenta, index, 0, keepdims=False)
    anchor_new, momentum = nesterov(summed / replicas, anchor, previous)
    new_anchors = lax.dynamic_update_index_in_dim(anchors, anchor_new, index, 0)
    new_momenta = lax.dynamic_update_index_in_dim(momenta, momentum, index, 0)
    merged_shard = merge_weight * local_fragment[0] + (1.0 - merge_weight) * anchor_new
    sent = merged_shard.astype(jnp.bfloat16)
    got = [sent] + [swapped(sent, "node", NODES, 2 * m) for m in range(1, CHIPS)]
    got = after(jnp.stack(got), back[0][1])
    other = after(swapped(got, "node", NODES, 1), back[1][0])
    merged = jnp.zeros((NODES, sent.shape[0]), f32)
    for m in range(CHIPS):
        for block, at in ((got[m], core), (other[m], 1 - core)):
            merged = lax.dynamic_update_index_in_dim(
                merged, block.astype(f32), (chip ^ m) * 2 + at, 0
            )
    return (
        new_weight[None],
        new_moment[None],
        new_second[None],
        grad_attention,
        new_anchors,
        new_momenta,
        merged.reshape(1, -1),
    )


def solution(mesh):
    return jax.shard_map(
        on_device,
        mesh=mesh,
        in_specs=(
            P(("rep", "node"), None),
            P(("rep", "node"), None),
            P(("rep", "node")),
            P("rep", "node", None),
            P("rep", "node", None),
            P("rep", "node", None),
            P("rep", None),
            P(),
            P("rep", "node", None),
            P(None, "node"),
            P(None, "node"),
            P("rep", "node"),
        ),
        out_specs=(
            P("rep", "node", None),
            P("rep", "node", None),
            P("rep", "node", None),
            P(("rep", "node"), None),
            P(None, "node"),
            P(None, "node"),
            P("rep", None),
        ),
        check_vma=False,
    )
```

```python
import jax
import jax.numpy as jnp
from jax import lax
from jax.sharding import PartitionSpec as P

beta_one = 0.9
beta_two = 0.95
adam_eps = 1e-08
inner_rate = 0.001
decay_rate = 0.1
inner_step = 10.0
outer_momentum = 0.9
outer_rate = 0.7
merge_weight = 0.5

NODES = 8
CHIPS = 4
HALVES = 2

def links(*pairs):
    return [(2 * a + core, 2 * b + core) for a, b in pairs for core in range(2)]


RING = links((0, 1), (1, 2), (2, 3), (3, 0))


def adamw(weight, moment, second, gradient):
    moment_new = beta_one * moment + (1.0 - beta_one) * gradient
    second_new = beta_two * second + (1.0 - beta_two) * gradient * gradient
    moment_hat = moment_new / (1.0 - beta_one**inner_step)
    second_hat = second_new / (1.0 - beta_two**inner_step)
    master = weight.astype(jnp.float32)
    updated = master - inner_rate * (
        moment_hat / (jnp.sqrt(second_hat) + adam_eps) + decay_rate * master
    )
    return (updated.astype(jnp.bfloat16), moment_new, second_new)


def nesterov(average, anchor, previous):
    momentum = outer_momentum * previous + average
    anchor_new = anchor - outer_rate * (average + outer_momentum * momentum)
    return (anchor_new, momentum)


def after(value, *others):
    return lax.optimization_barrier((value, *others))[0]


def swapped(value, axis, size, mask):
    return lax.ppermute(value, axis, [(a, a ^ mask) for a in range(size)])


def on_device(
    attention,
    cotangent,
    token_ids,
    out_weight,
    moment,
    second,
    norm_gain,
    frag_index,
    outer_delta,
    anchors,
    momenta,
    local_fragment,
):
    node = lax.axis_index("node")
    replicas = lax.axis_size("rep")
    chip, core = node // 2, node % 2
    weight_shard = out_weight[0]
    second_moment = second[0]
    gain = 1.0 + norm_gain[0]
    rows, width = weight_shard.shape
    tokens, features = attention.shape
    span = width // HALVES
    f32 = jnp.float32
    part = rows // HALVES

    def send(value, pairs):
        return lax.ppermute(value, "node", pairs)

    def cross(value):
        return swapped(value, "node", NODES, 1)

    def columns(owner):
        return lax.dynamic_slice(attention, (0, owner * rows), (tokens, rows))

    turns = [(chip - step) % CHIPS for step in range(1, CHIPS + 1)]
    own_cols = [columns(c * 2 + core) for c in turns]
    twin_cols = [columns(c * 2 + 1 - core) for c in turns]
    own_t = [jnp.transpose(block) for block in own_cols]
    lent = cross(jnp.concatenate(twin_cols, axis=1))

    delta = outer_delta.reshape(-1)
    shard = delta.shape[0] // NODES

    def take(owner):
        return lax.dynamic_slice(delta, (owner * shard,), (shard,))

    give = [take((chip ^ m) * 2 + 1 - core).astype(jnp.bfloat16) for m in range(CHIPS)]
    got = swapped(jnp.concatenate(give), "node", NODES, 1)
    held = [
        take((chip ^ m) * 2 + core) + got[m * shard : (m + 1) * shard].astype(f32)
        for m in range(CHIPS)
    ]

    def product(total, left, right):
        return total + jnp.dot(left, right, preferred_element_type=f32)

    halves = [weight_shard[h * part : (h + 1) * part] for h in range(HALVES)]
    own_twin = cross(weight_shard)
    lent, own_twin, *held = lax.optimization_barrier((lent, own_twin, *held))
    away = [
        swapped(held[m].astype(jnp.bfloat16), "node", NODES, 2 * m) for m in range(1, CHIPS)
    ]
    projected = product(jnp.zeros((tokens, width), f32), own_cols[3], weight_shard)
    projected = product(projected, twin_cols[3], own_twin)

    one, two = send(halves[0], RING), send(after(halves[1], got), RING)
    one_twin = cross(one)
    two, projected, *away = lax.optimization_barrier((two, projected, *away))
    two_twin = cross(two)
    total = (held[0] + away[0].astype(f32)) + (away[1].astype(f32) + away[2].astype(f32))
    total = after(total, two_twin)
    other = swapped(total, "rep", replicas, 1)
    pairs = [jnp.concatenate([one, two, one_twin, two_twin])]
    both_cols = [jnp.concatenate(pair, axis=1) for pair in zip(own_cols, twin_cols)]

    one, two = send(one, RING), send(two, RING)
    one, other = lax.optimization_barrier((one, other))
    one_twin = cross(one)
    total = after(total + other, one_twin)
    other = swapped(total, "rep", replicas, 2)
    projected = product(projected, both_cols[0], pairs[0])
    two, other, projected = lax.optimization_barrier((two, other, projected))
    two_twin = cross(two)
    total = after(total + other, two_twin)
    other = swapped(total, "rep", replicas, 4)
    pairs.append(jnp.concatenate([one, two, one_twin, two_twin]))

    one, two = send(one, RING), send(two, RING)
    one, other = lax.optimization_barrier((one, other))
    one_twin = cross(one)
    total = after(total + other, one_twin)
    other = swapped(total, "rep", replicas, 8)
    projected = product(projected, both_cols[1], pairs[1])
    projected = product(projected, own_cols[2][:, :part], one)
    projected = product(projected, twin_cols[2][:, :part], one_twin)
    two, other, projected = lax.optimization_barrier((two, other, projected))
    two_twin = cross(two)
    total = total + other
    projected = product(projected, own_cols[2][:, part:], two)
    projected = product(projected, twin_cols[2][:, part:], two_twin)
    pairs.append(jnp.concatenate([one, two, one_twin, two_twin]))
    pairs.append(jnp.concatenate([weight_shard, own_twin]))
    rounded = after(total, two).astype(jnp.bfloat16)
    other = swapped(rounded, "rep", replicas, 16)

    loss_mask = (token_ids != 0).astype(f32)
    meansq = jnp.mean(projected * projected, axis=-1, keepdims=True)
    scale = lax.rsqrt(meansq + 1e-06)
    weighted = cotangent.astype(f32) * loss_mask[:, None] * gain
    inner = jnp.mean(weighted * projected, axis=-1, keepdims=True)
    curve = scale * scale * scale * inner
    ranges = [slice(h * span, (h + 1) * span) for h in range(HALVES)]
    pieces = [
        (scale * weighted[:, at] - curve * projected[:, at]).astype(jnp.bfloat16)
        for at in ranges
    ]

    dtwin = [cross(piece) for piece in pieces]
    lent_t = [jnp.transpose(lent[:, n * rows : (n + 1) * rows]) for n in range(CHIPS)]

    def partial(step, h, *event):
        mine = after(own_t[step], dtwin[h], *event)
        return jnp.dot(mine, pieces[h], preferred_element_type=f32) + jnp.dot(
            lent_t[step], dtwin[h], preferred_element_type=f32
        )

    both = range(HALVES)
    travelling, back = [], []
    for h in both:
        travelling.append(partial(0, h, *travelling).astype(jnp.bfloat16))
    opening = list(travelling)
    for step in range(1, CHIPS):
        arrived = [send(piece, RING) for piece in travelling]
        back.append(arrived)
        sums = []
        for h in both:
            event = [arrived[0]] if h == 0 else [travelling[0]]
            sums.append(partial(step, h, *event) + arrived[h].astype(f32))
            travelling[h] = sums[h].astype(jnp.bfloat16)
    gradient = jnp.concatenate(sums, axis=1)
    new_weight, new_moment, new_second = adamw(
        weight_shard, moment[0], second_moment, gradient
    )

    grad_attention = jnp.zeros((tokens, features), jnp.bfloat16)
    contract = (((1,), (1,)), ((), ()))
    dprojected = jnp.concatenate(pieces, axis=1)
    for which, owner in enumerate(turns):
        held_back = after(dprojected, back[1 + which // 2][0])
        block = lax.dot_general(
            held_back, pairs[which], contract, preferred_element_type=f32
        ).astype(jnp.bfloat16)
        for n, at in enumerate((core, 1 - core)):
            grad_attention = lax.dynamic_update_slice(
                grad_attention,
                block[:, n * rows : (n + 1) * rows],
                (0, (owner * 2 + at) * rows),
            )

    summed = rounded.astype(f32) + other.astype(f32)
    index = frag_index[0]
    anchor = lax.dynamic_index_in_dim(after(anchors, two), index, 0, keepdims=False)
    previous = lax.dynamic_index_in_dim(after(momenta, two), index, 0, keepdims=False)
    anchor_new, momentum = nesterov(summed / replicas, anchor, previous)
    due = jnp.arange(anchors.shape[0])[:, None] == index
    new_anchors = jnp.where(due, anchor_new[None], anchors)
    new_momenta = jnp.where(due, momentum[None], momenta)
    merged_shard = merge_weight * local_fragment[0] + (1.0 - merge_weight) * anchor_new
    sent = after(merged_shard.astype(jnp.bfloat16), *opening)
    parts = [swapped(sent, "node", NODES, 2 * m) for m in range(1, CHIPS)]
    parts = jnp.concatenate([sent, *after(parts, back[1][0])])
    other = cross(parts)
    merged = jnp.zeros((NODES * shard,), f32)
    for m in range(CHIPS):
        for block, at in ((parts, core), (other, 1 - core)):
            piece = block[m * shard : (m + 1) * shard].astype(f32)
            merged = lax.dynamic_update_slice(merged, piece, (((chip ^ m) * 2 + at) * shard,))
    return (
        new_weight[None],
        new_moment[None],
        new_second[None],
        grad_attention,
        new_anchors,
        new_momenta,
        merged.reshape(1, -1),
    )


def solution(mesh):
    return jax.shard_map(
        on_device,
        mesh=mesh,
        in_specs=(
            P(("rep", "node"), None),
            P(("rep", "node"), None),
            P(("rep", "node")),
            P("rep", "node", None),
            P("rep", "node", None),
            P("rep", "node", None),
            P("rep", None),
            P(),
            P("rep", "node", None),
            P(None, "node"),
            P(None, "node"),
            P("rep", "node"),
        ),
        out_specs=(
            P("rep", "node", None),
            P("rep", "node", None),
            P("rep", "node", None),
            P(("rep", "node"), None),
            P(None, "node"),
            P(None, "node"),
            P("rep", None),
        ),
        check_vma=False,
    )
```

```python
import jax
import jax.numpy as jnp
from jax import lax
from jax.sharding import PartitionSpec as P

beta_one = 0.9
beta_two = 0.95
adam_eps = 1e-08
inner_rate = 0.001
decay_rate = 0.1
inner_step = 10.0
outer_momentum = 0.9
outer_rate = 0.7
merge_weight = 0.5

NODES = 8
CHIPS = 4
HALVES = 2

def links(*pairs):
    return [(2 * a + core, 2 * b + core) for a, b in pairs for core in range(2)]


RING = links((0, 1), (1, 2), (2, 3), (3, 0))


def adamw(weight, moment, second, gradient):
    moment_new = beta_one * moment + (1.0 - beta_one) * gradient
    second_new = beta_two * second + (1.0 - beta_two) * gradient * gradient
    moment_hat = moment_new / (1.0 - beta_one**inner_step)
    second_hat = second_new / (1.0 - beta_two**inner_step)
    master = weight.astype(jnp.float32)
    updated = master - inner_rate * (
        moment_hat / (jnp.sqrt(second_hat) + adam_eps) + decay_rate * master
    )
    return (updated.astype(jnp.bfloat16), moment_new, second_new)


def nesterov(average, anchor, previous):
    momentum = outer_momentum * previous + average
    anchor_new = anchor - outer_rate * (average + outer_momentum * momentum)
    return (anchor_new, momentum)


def after(value, *others):
    return lax.optimization_barrier((value, *others))[0]


def swapped(value, axis, size, mask):
    return lax.ppermute(value, axis, [(a, a ^ mask) for a in range(size)])


def on_device(
    attention,
    cotangent,
    token_ids,
    out_weight,
    moment,
    second,
    norm_gain,
    frag_index,
    outer_delta,
    anchors,
    momenta,
    local_fragment,
):
    node = lax.axis_index("node")
    replicas = lax.axis_size("rep")
    chip, core = node // 2, node % 2
    weight_shard = out_weight[0]
    second_moment = second[0]
    gain = 1.0 + norm_gain[0]
    rows, width = weight_shard.shape
    tokens, features = attention.shape
    span = width // HALVES
    f32 = jnp.float32
    part = rows // HALVES

    def send(value, pairs):
        return lax.ppermute(value, "node", pairs)

    def cross(value):
        return swapped(value, "node", NODES, 1)

    delta = outer_delta.reshape(-1)
    shard = delta.shape[0] // NODES

    def take(owner):
        return lax.dynamic_slice(delta, (owner * shard,), (shard,))

    give = [take((chip ^ m) * 2 + 1 - core).astype(jnp.bfloat16) for m in range(CHIPS)]
    got = swapped(jnp.concatenate(give), "node", NODES, 1)
    held = [
        take((chip ^ m) * 2 + core) + got[m * shard : (m + 1) * shard].astype(f32)
        for m in range(CHIPS)
    ]

    def product(total, left, right):
        return total + jnp.dot(left, right, preferred_element_type=f32)

    halves = [weight_shard[h * part : (h + 1) * part] for h in range(HALVES)]
    away = [
        swapped(held[m].astype(jnp.bfloat16), "node", NODES, 2 * m) for m in range(1, CHIPS)
    ]

    one = send(halves[0], RING)
    two = after(send(after(halves[1], got), RING), one)
    one_twin = cross(one)
    two, *away = lax.optimization_barrier((two, *away))
    two_twin = cross(two)
    attention = after(attention, two)

    def columns(owner):
        return lax.dynamic_slice(attention, (0, owner * rows), (tokens, rows))

    turns = [(chip - step) % CHIPS for step in range(1, CHIPS + 1)]
    own_cols = [columns(c * 2 + core) for c in turns]
    twin_cols = [columns(c * 2 + 1 - core) for c in turns]
    own_t = [jnp.transpose(block) for block in own_cols]
    lent = cross(jnp.concatenate(twin_cols, axis=1))

    total = (held[0] + away[0].astype(f32)) + (away[1].astype(f32) + away[2].astype(f32))
    total = after(total, two_twin)
    total = total + swapped(total, "rep", replicas, 1)
    total = total + swapped(total, "rep", replicas, 2)
    own_twin = cross(after(weight_shard, two))
    projected = product(jnp.zeros((tokens, width), f32), own_cols[3], weight_shard)
    projected = product(projected, twin_cols[3], own_twin)
    pairs = [jnp.concatenate([one, two, one_twin, two_twin])]
    both_cols = [jnp.concatenate(pair, axis=1) for pair in zip(own_cols, twin_cols)]

    one, two = after(send(one, RING), two), send(two, RING)
    one_twin = cross(one)
    two, total, projected, lent = lax.optimization_barrier(
        (after(two, one), total, projected, lent)
    )
    two_twin = cross(two)
    total = after(total, two_twin)
    total = total + swapped(total, "rep", replicas, 4)
    total = total + swapped(total, "rep", replicas, 8)
    projected = product(projected, both_cols[0], pairs[0])
    pairs.append(jnp.concatenate([one, two, one_twin, two_twin]))

    one, two = after(send(one, RING), two), send(two, RING)
    one_twin = cross(one)
    projected = product(projected, both_cols[1], pairs[1])
    projected = product(projected, own_cols[2][:, :part], one)
    projected = product(projected, twin_cols[2][:, :part], one_twin)
    two, total, projected = lax.optimization_barrier((two, total, projected))
    two_twin = cross(two)
    projected = product(projected, own_cols[2][:, part:], two)
    projected = product(projected, twin_cols[2][:, part:], two_twin)
    pairs.append(jnp.concatenate([one, two, one_twin, two_twin]))
    pairs.append(jnp.concatenate([weight_shard, own_twin]))
    loss_mask = (token_ids != 0).astype(f32)
    meansq = jnp.mean(projected * projected, axis=-1, keepdims=True)
    scale = lax.rsqrt(meansq + 1e-06)
    weighted = cotangent.astype(f32) * loss_mask[:, None] * gain
    inner = jnp.mean(weighted * projected, axis=-1, keepdims=True)
    curve = scale * scale * scale * inner
    ranges = [slice(h * span, (h + 1) * span) for h in range(HALVES)]
    pieces = [
        (scale * weighted[:, at] - curve * projected[:, at]).astype(jnp.bfloat16)
        for at in ranges
    ]

    dtwin = [cross(piece) for piece in pieces]
    lent_t = [jnp.transpose(lent[:, n * rows : (n + 1) * rows]) for n in range(CHIPS)]

    def partial(step, h, *event):
        mine = after(own_t[step], dtwin[h], *event)
        return jnp.dot(mine, pieces[h], preferred_element_type=f32) + jnp.dot(
            lent_t[step], dtwin[h], preferred_element_type=f32
        )

    both = range(HALVES)
    travelling, back = [], []
    for h in both:
        travelling.append(partial(0, h, *travelling).astype(jnp.bfloat16))
    sent = [list(travelling)]
    for step in range(1, CHIPS):
        arrived = [send(piece, RING) for piece in travelling]
        back.append(arrived)
        sums = []
        for h in both:
            event = [arrived[h], travelling[1 - h]]
            sums.append(partial(step, h, *event) + arrived[h].astype(f32))
            travelling[h] = sums[h].astype(jnp.bfloat16)
        sent.append(list(travelling))
    gradient = jnp.concatenate(sums, axis=1)
    new_weight, new_moment, new_second = adamw(
        weight_shard, moment[0], second_moment, gradient
    )

    grad_attention = jnp.zeros((tokens, features), jnp.bfloat16)
    contract = (((1,), (1,)), ((), ()))
    dprojected = jnp.concatenate(pieces, axis=1)
    for which, owner in enumerate(turns):
        held_back = after(dprojected, sent[1 + which // 2][1])
        block = lax.dot_general(
            held_back, pairs[which], contract, preferred_element_type=f32
        ).astype(jnp.bfloat16)
        for n, at in enumerate((core, 1 - core)):
            grad_attention = lax.dynamic_update_slice(
                grad_attention,
                block[:, n * rows : (n + 1) * rows],
                (0, (owner * 2 + at) * rows),
            )

    rounded = after(total.astype(jnp.bfloat16), *sent[0])
    other = after(swapped(rounded, "rep", replicas, 16), sent[1][1])
    summed = rounded.astype(f32) + other.astype(f32)
    index = frag_index[0]
    anchor = lax.dynamic_index_in_dim(after(anchors, *sent[0]), index, 0, keepdims=False)
    previous = lax.dynamic_index_in_dim(after(momenta, *sent[0]), index, 0, keepdims=False)
    anchor_new, momentum = nesterov(summed / replicas, anchor, previous)
    due = jnp.arange(anchors.shape[0])[:, None] == index
    new_anchors = jnp.where(due, anchor_new[None], anchors)
    new_momenta = jnp.where(due, momentum[None], momenta)
    merged_shard = merge_weight * local_fragment[0] + (1.0 - merge_weight) * anchor_new
    parts = merged_shard.astype(jnp.bfloat16)
    parts = jnp.concatenate([parts, after(swapped(parts, "node", NODES, 2), sent[2][1])])
    parts = jnp.concatenate([parts, swapped(parts, "node", NODES, 4)])
    other = cross(parts)
    merged = jnp.zeros((NODES * shard,), f32)
    for m in range(CHIPS):
        for block, at in ((parts, core), (other, 1 - core)):
            piece = block[m * shard : (m + 1) * shard].astype(f32)
            merged = lax.dynamic_update_slice(merged, piece, (((chip ^ m) * 2 + at) * shard,))
    return (
        new_weight[None],
        new_moment[None],
        new_second[None],
        grad_attention,
        new_anchors,
        new_momenta,
        merged.reshape(1, -1),
    )


def solution(mesh):
    return jax.shard_map(
        on_device,
        mesh=mesh,
        in_specs=(
            P(("rep", "node"), None),
            P(("rep", "node"), None),
            P(("rep", "node")),
            P("rep", "node", None),
            P("rep", "node", None),
            P("rep", "node", None),
            P("rep", None),
            P(),
            P("rep", "node", None),
            P(None, "node"),
            P(None, "node"),
            P("rep", "node"),
        ),
        out_specs=(
            P("rep", "node", None),
            P("rep", "node", None),
            P("rep", "node", None),
            P(("rep", "node"), None),
            P(None, "node"),
            P(None, "node"),
            P("rep", None),
        ),
        check_vma=False,
    )
```

```python
import jax
import jax.numpy as jnp
from jax import lax
from jax.sharding import PartitionSpec as P

beta_one = 0.9
beta_two = 0.95
adam_eps = 1e-08
inner_rate = 0.001
decay_rate = 0.1
inner_step = 10.0
outer_momentum = 0.9
outer_rate = 0.7
merge_weight = 0.5

NODES = 8
CHIPS = 4
HALVES = 2

def links(*pairs):
    return [(2 * a + core, 2 * b + core) for a, b in pairs for core in range(2)]


RING = links((0, 1), (1, 2), (2, 3), (3, 0))


def adamw(weight, moment, second, gradient):
    moment_new = beta_one * moment + (1.0 - beta_one) * gradient
    second_new = beta_two * second + (1.0 - beta_two) * gradient * gradient
    moment_hat = moment_new / (1.0 - beta_one**inner_step)
    second_hat = second_new / (1.0 - beta_two**inner_step)
    master = weight.astype(jnp.float32)
    updated = master - inner_rate * (
        moment_hat / (jnp.sqrt(second_hat) + adam_eps) + decay_rate * master
    )
    return (updated.astype(jnp.bfloat16), moment_new, second_new)


def nesterov(average, anchor, previous):
    momentum = outer_momentum * previous + average
    anchor_new = anchor - outer_rate * (average + outer_momentum * momentum)
    return (anchor_new, momentum)


def after(value, *others):
    return lax.optimization_barrier((value, *others))[0]


def swapped(value, axis, size, mask):
    return lax.ppermute(value, axis, [(a, a ^ mask) for a in range(size)])


def on_device(
    attention,
    cotangent,
    token_ids,
    out_weight,
    moment,
    second,
    norm_gain,
    frag_index,
    outer_delta,
    anchors,
    momenta,
    local_fragment,
):
    node = lax.axis_index("node")
    replicas = lax.axis_size("rep")
    chip, core = node // 2, node % 2
    weight_shard = out_weight[0]
    second_moment = second[0]
    gain = 1.0 + norm_gain[0]
    rows, width = weight_shard.shape
    tokens, features = attention.shape
    span = width // HALVES
    f32 = jnp.float32
    part = rows // HALVES

    def send(value, pairs):
        return lax.ppermute(value, "node", pairs)

    def cross(value):
        return swapped(value, "node", NODES, 1)

    halves = [weight_shard[h * part : (h + 1) * part] for h in range(HALVES)]
    delta = after(outer_delta.reshape(-1), *halves)
    shard = delta.shape[0] // NODES

    def take(owner):
        return lax.dynamic_slice(delta, (owner * shard,), (shard,))

    give = [take((chip ^ m) * 2 + 1 - core).astype(jnp.bfloat16) for m in range(CHIPS)]
    got = swapped(jnp.concatenate(give), "node", NODES, 1)
    held = [
        take((chip ^ m) * 2 + core) + got[m * shard : (m + 1) * shard].astype(f32)
        for m in range(CHIPS)
    ]

    def product(total, left, right):
        return total + jnp.dot(left, right, preferred_element_type=f32)

    away = [
        swapped(held[m].astype(jnp.bfloat16), "node", NODES, 2 * m) for m in range(1, CHIPS)
    ]

    one = send(halves[0], RING)
    two = after(send(after(halves[1], got), RING), one)
    one_twin = cross(one)
    two, *away = lax.optimization_barrier((two, *away))
    two_twin = cross(two)
    attention = after(attention, two)

    def columns(owner):
        return lax.dynamic_slice(attention, (0, owner * rows), (tokens, rows))

    turns = [(chip - step) % CHIPS for step in range(1, CHIPS + 1)]
    own_cols = [columns(c * 2 + core) for c in turns]
    twin_cols = [columns(c * 2 + 1 - core) for c in turns]
    own_t = [jnp.transpose(block) for block in own_cols]
    lent = cross(jnp.concatenate(twin_cols, axis=1))

    total = (held[0] + away[0].astype(f32)) + (away[1].astype(f32) + away[2].astype(f32))
    total = total + swapped(total, "rep", replicas, 1)
    total = total + swapped(total, "rep", replicas, 2)
    own_twin = cross(after(weight_shard, two))
    projected = product(jnp.zeros((tokens, width), f32), own_cols[3], weight_shard)
    projected = product(projected, twin_cols[3], own_twin)
    pairs = [jnp.concatenate([one, two, one_twin, two_twin])]
    both_cols = [jnp.concatenate(pair, axis=1) for pair in zip(own_cols, twin_cols)]

    one, two = after(send(one, RING), two), send(two, RING)
    one, total = lax.optimization_barrier((one, total))
    one_twin = cross(one)
    total = total + swapped(total, "rep", replicas, 4)
    total = total + swapped(total, "rep", replicas, 8)
    passed_two = after(two, one)
    two, total, projected, lent = lax.optimization_barrier(
        (passed_two, total, projected, lent)
    )
    two_twin = cross(two)
    projected = product(projected, both_cols[0], pairs[0])
    pairs.append(jnp.concatenate([one, two, one_twin, two_twin]))

    one, two = after(send(one, RING), two), send(passed_two, RING)
    one_twin = cross(one)
    projected = product(projected, both_cols[1], pairs[1])
    projected = product(projected, own_cols[2][:, :part], one)
    projected = product(projected, twin_cols[2][:, :part], one_twin)
    two, total, projected = lax.optimization_barrier((two, total, projected))
    two_twin = cross(two)
    projected = product(projected, own_cols[2][:, part:], two)
    projected = product(projected, twin_cols[2][:, part:], two_twin)
    pairs.append(jnp.concatenate([one, two, one_twin, two_twin]))
    pairs.append(jnp.concatenate([weight_shard, own_twin]))
    loss_mask = (token_ids != 0).astype(f32)
    meansq = jnp.mean(projected * projected, axis=-1, keepdims=True)
    scale = lax.rsqrt(meansq + 1e-06)
    weighted = cotangent.astype(f32) * loss_mask[:, None] * gain
    inner = jnp.mean(weighted * projected, axis=-1, keepdims=True)
    curve = scale * scale * scale * inner
    ranges = [slice(h * span, (h + 1) * span) for h in range(HALVES)]
    pieces = [
        (scale * weighted[:, at] - curve * projected[:, at]).astype(jnp.bfloat16)
        for at in ranges
    ]

    dtwin = [cross(piece) for piece in pieces]
    lent_t = [jnp.transpose(lent[:, n * rows : (n + 1) * rows]) for n in range(CHIPS)]

    def partial(step, h, *event):
        mine = after(own_t[step], dtwin[h], *event)
        return jnp.dot(mine, pieces[h], preferred_element_type=f32) + jnp.dot(
            lent_t[step], dtwin[h], preferred_element_type=f32
        )

    both = range(HALVES)
    travelling, back = [], []
    for h in both:
        travelling.append(partial(0, h, *travelling).astype(jnp.bfloat16))
    sent = [list(travelling)]
    for step in range(1, CHIPS):
        arrived = [send(piece, RING) for piece in travelling]
        back.append(arrived)
        sums = []
        for h in both:
            event = [arrived[h], travelling[1 - h]]
            sums.append(partial(step, h, *event) + arrived[h].astype(f32))
            travelling[h] = sums[h].astype(jnp.bfloat16)
        sent.append(list(travelling))
    gradient = jnp.concatenate(sums, axis=1)
    new_weight, new_moment, new_second = adamw(
        weight_shard, moment[0], second_moment, gradient
    )

    grad_attention = jnp.zeros((tokens, features), jnp.bfloat16)
    contract = (((1,), (1,)), ((), ()))
    dprojected = jnp.concatenate(pieces, axis=1)
    for which, owner in enumerate(turns):
        held_back = after(dprojected, sent[1 + which // 2][1])
        block = lax.dot_general(
            held_back, pairs[which], contract, preferred_element_type=f32
        ).astype(jnp.bfloat16)
        for n, at in enumerate((core, 1 - core)):
            grad_attention = lax.dynamic_update_slice(
                grad_attention,
                block[:, n * rows : (n + 1) * rows],
                (0, (owner * 2 + at) * rows),
            )

    rounded = after(total.astype(jnp.bfloat16), *sent[0])
    other = after(swapped(rounded, "rep", replicas, 16), sent[1][1])
    summed = rounded.astype(f32) + other.astype(f32)
    index = frag_index[0]
    anchor = lax.dynamic_index_in_dim(after(anchors, *sent[0]), index, 0, keepdims=False)
    previous = lax.dynamic_index_in_dim(after(momenta, *sent[0]), index, 0, keepdims=False)
    anchor_new, momentum = nesterov(summed / replicas, anchor, previous)
    due = jnp.arange(anchors.shape[0])[:, None] == index
    new_anchors = jnp.where(due, anchor_new[None], anchors)
    new_momenta = jnp.where(due, momentum[None], momenta)
    merged_shard = merge_weight * local_fragment[0] + (1.0 - merge_weight) * anchor_new
    parts = merged_shard.astype(jnp.bfloat16)
    parts = jnp.concatenate([parts, after(swapped(parts, "node", NODES, 2), sent[2][1])])
    parts = jnp.concatenate([parts, swapped(parts, "node", NODES, 4)])
    other = cross(parts)
    merged = jnp.zeros((NODES * shard,), f32)
    for m in range(CHIPS):
        for block, at in ((parts, core), (other, 1 - core)):
            piece = block[m * shard : (m + 1) * shard].astype(f32)
            merged = lax.dynamic_update_slice(merged, piece, (((chip ^ m) * 2 + at) * shard,))
    return (
        new_weight[None],
        new_moment[None],
        new_second[None],
        grad_attention,
        new_anchors,
        new_momenta,
        merged.reshape(1, -1),
    )


def solution(mesh):
    return jax.shard_map(
        on_device,
        mesh=mesh,
        in_specs=(
            P(("rep", "node"), None),
            P(("rep", "node"), None),
            P(("rep", "node")),
            P("rep", "node", None),
            P("rep", "node", None),
            P("rep", "node", None),
            P("rep", None),
            P(),
            P("rep", "node", None),
            P(None, "node"),
            P(None, "node"),
            P("rep", "node"),
        ),
        out_specs=(
            P("rep", "node", None),
            P("rep", "node", None),
            P("rep", "node", None),
            P(("rep", "node"), None),
            P(None, "node"),
            P(None, "node"),
            P("rep", None),
        ),
        check_vma=False,
    )
```

```python
import jax
import jax.numpy as jnp
from jax import lax
from jax.sharding import PartitionSpec as P

beta_one = 0.9
beta_two = 0.95
adam_eps = 1e-08
inner_rate = 0.001
decay_rate = 0.1
inner_step = 10.0
outer_momentum = 0.9
outer_rate = 0.7
merge_weight = 0.5

NODES = 8
CHIPS = 4
HALVES = 2

def links(*pairs):
    return [(2 * a + core, 2 * b + core) for a, b in pairs for core in range(2)]


RING = links((0, 1), (1, 2), (2, 3), (3, 0))


def adamw(weight, moment, second, gradient):
    moment_new = beta_one * moment + (1.0 - beta_one) * gradient
    second_new = beta_two * second + (1.0 - beta_two) * gradient * gradient
    moment_hat = moment_new * (inner_rate / (1.0 - beta_one**inner_step))
    second_hat = second_new * (1.0 / (1.0 - beta_two**inner_step))
    master = weight.astype(jnp.float32)
    step = moment_hat / (jnp.sqrt(second_hat) + adam_eps)
    updated = master * (1.0 - inner_rate * decay_rate) - step
    return (updated.astype(jnp.bfloat16), moment_new, second_new)


def nesterov(average, anchor, previous):
    momentum = outer_momentum * previous + average
    anchor_new = anchor - outer_rate * (average + outer_momentum * momentum)
    return (anchor_new, momentum)


def after(value, *others):
    return lax.optimization_barrier((value, *others))[0]


def swapped(value, axis, size, mask):
    return lax.ppermute(value, axis, [(a, a ^ mask) for a in range(size)])


def on_device(
    attention,
    cotangent,
    token_ids,
    out_weight,
    moment,
    second,
    norm_gain,
    frag_index,
    outer_delta,
    anchors,
    momenta,
    local_fragment,
):
    node = lax.axis_index("node")
    replicas = lax.axis_size("rep")
    chip, core = node // 2, node % 2
    weight_shard = out_weight[0]
    second_moment = second[0]
    gain = 1.0 + norm_gain[0]
    rows, width = weight_shard.shape
    tokens, features = attention.shape
    span = width // HALVES
    f32 = jnp.float32
    part = rows // HALVES

    def send(value, pairs):
        return lax.ppermute(value, "node", pairs)

    def cross(value):
        return swapped(value, "node", NODES, 1)

    halves = [weight_shard[h * part : (h + 1) * part] for h in range(HALVES)]
    delta = after(outer_delta.reshape(-1), *halves)
    shard = delta.shape[0] // NODES

    def take(owner):
        return lax.dynamic_slice(delta, (owner * shard,), (shard,))

    give = [take((chip ^ m) * 2 + 1 - core).astype(jnp.bfloat16) for m in range(CHIPS)]
    got = swapped(jnp.concatenate(give), "node", NODES, 1)
    held = [
        take((chip ^ m) * 2 + core) + got[m * shard : (m + 1) * shard].astype(f32)
        for m in range(CHIPS)
    ]

    def product(total, left, right):
        return total + jnp.dot(left, right, preferred_element_type=f32)

    away = [
        swapped(held[m].astype(jnp.bfloat16), "node", NODES, 2 * m) for m in range(1, CHIPS)
    ]

    one = send(halves[0], RING)
    two = after(send(after(halves[1], got), RING), one)
    one_twin = cross(one)
    two, *away = lax.optimization_barrier((two, *away))
    two_twin = cross(two)
    attention = after(attention, two)

    def columns(owner):
        return lax.dynamic_slice(attention, (0, owner * rows), (tokens, rows))

    turns = [(chip - step) % CHIPS for step in range(1, CHIPS + 1)]
    own_cols = [columns(c * 2 + core) for c in turns]
    twin_cols = [columns(c * 2 + 1 - core) for c in turns]
    own_t = [jnp.transpose(block) for block in own_cols]
    lent = cross(jnp.concatenate(twin_cols, axis=1))

    total = (held[0] + away[0].astype(f32)) + (away[1].astype(f32) + away[2].astype(f32))
    total = total + swapped(total, "rep", replicas, 1)
    total = total + swapped(total, "rep", replicas, 2)
    own_twin = cross(after(weight_shard, two))
    projected = product(jnp.zeros((tokens, width), f32), own_cols[3], weight_shard)
    projected = product(projected, twin_cols[3], own_twin)
    pairs = [jnp.concatenate([one, two, one_twin, two_twin])]
    both_cols = [jnp.concatenate(pair, axis=1) for pair in zip(own_cols, twin_cols)]

    one, two = after(send(one, RING), two), send(two, RING)
    one, total = lax.optimization_barrier((one, total))
    one_twin = cross(one)
    total = total + swapped(total, "rep", replicas, 4)
    total = total + swapped(total, "rep", replicas, 8)
    passed_two = after(two, one)
    two, total, projected, lent = lax.optimization_barrier(
        (passed_two, total, projected, lent)
    )
    two_twin = cross(two)
    projected = product(projected, both_cols[0], pairs[0])
    pairs.append(jnp.concatenate([one, two, one_twin, two_twin]))

    one, two = after(send(one, RING), two), send(passed_two, RING)
    one_twin = cross(one)
    projected = product(projected, both_cols[1], pairs[1])
    projected = product(projected, own_cols[2][:, :part], one)
    projected = product(projected, twin_cols[2][:, :part], one_twin)
    two, total, projected = lax.optimization_barrier((two, total, projected))
    two_twin = cross(two)
    projected = product(projected, own_cols[2][:, part:], two)
    projected = product(projected, twin_cols[2][:, part:], two_twin)
    pairs.append(jnp.concatenate([one, two, one_twin, two_twin]))
    pairs.append(jnp.concatenate([weight_shard, own_twin]))
    loss_mask = (token_ids != 0).astype(f32)
    meansq = jnp.mean(projected * projected, axis=-1, keepdims=True)
    scale = lax.rsqrt(meansq + 1e-06)
    weighted = cotangent.astype(f32) * loss_mask[:, None] * gain
    inner = jnp.mean(weighted * projected, axis=-1, keepdims=True)
    curve = scale * scale * scale * inner
    ranges = [slice(h * span, (h + 1) * span) for h in range(HALVES)]
    pieces = [
        (scale * weighted[:, at] - curve * projected[:, at]).astype(jnp.bfloat16)
        for at in ranges
    ]

    dtwin = [cross(piece) for piece in pieces]
    lent_t = [jnp.transpose(lent[:, n * rows : (n + 1) * rows]) for n in range(CHIPS)]

    def partial(step, h, *event):
        mine = after(own_t[step], dtwin[h], *event)
        return jnp.dot(mine, pieces[h], preferred_element_type=f32) + jnp.dot(
            lent_t[step], dtwin[h], preferred_element_type=f32
        )

    both = range(HALVES)
    travelling, back = [], []
    for h in both:
        travelling.append(partial(0, h, *travelling).astype(jnp.bfloat16))
    sent = [list(travelling)]
    for step in range(1, CHIPS):
        arrived = [send(piece, RING) for piece in travelling]
        back.append(arrived)
        sums = []
        for h in both:
            event = [arrived[h], travelling[1 - h]]
            sums.append(partial(step, h, *event) + arrived[h].astype(f32))
            travelling[h] = sums[h].astype(jnp.bfloat16)
        sent.append(list(travelling))
    gradient = jnp.concatenate(sums, axis=1)
    new_weight, new_moment, new_second = adamw(
        weight_shard, moment[0], second_moment, gradient
    )

    grad_attention = jnp.zeros((tokens, features), jnp.bfloat16)
    contract = (((1,), (1,)), ((), ()))
    dprojected = jnp.concatenate(pieces, axis=1)
    for which, owner in enumerate(turns):
        held_back = after(dprojected, sent[1 + which // 2][1])
        block = lax.dot_general(
            held_back, pairs[which], contract, preferred_element_type=f32
        ).astype(jnp.bfloat16)
        for n, at in enumerate((core, 1 - core)):
            grad_attention = lax.dynamic_update_slice(
                grad_attention,
                block[:, n * rows : (n + 1) * rows],
                (0, (owner * 2 + at) * rows),
            )

    rounded = after(total.astype(jnp.bfloat16), *sent[0])
    other = after(swapped(rounded, "rep", replicas, 16), sent[1][1])
    summed = rounded.astype(f32) + other.astype(f32)
    index = frag_index[0]
    anchor = lax.dynamic_index_in_dim(after(anchors, *sent[0]), index, 0, keepdims=False)
    previous = lax.dynamic_index_in_dim(after(momenta, *sent[0]), index, 0, keepdims=False)
    anchor_new, momentum = nesterov(summed / replicas, anchor, previous)
    due = jnp.arange(anchors.shape[0])[:, None] == index
    new_anchors = jnp.where(due, anchor_new[None], anchors)
    new_momenta = jnp.where(due, momentum[None], momenta)
    merged_shard = merge_weight * local_fragment[0] + (1.0 - merge_weight) * anchor_new
    parts = merged_shard.astype(jnp.bfloat16)
    parts = jnp.concatenate([parts, after(swapped(parts, "node", NODES, 2), sent[2][1])])
    parts = jnp.concatenate([parts, swapped(parts, "node", NODES, 4)])
    other = cross(parts)
    merged = jnp.zeros((NODES * shard,), f32)
    for m in range(CHIPS):
        for block, at in ((parts, core), (other, 1 - core)):
            piece = block[m * shard : (m + 1) * shard].astype(f32)
            merged = lax.dynamic_update_slice(merged, piece, (((chip ^ m) * 2 + at) * shard,))
    return (
        new_weight[None],
        new_moment[None],
        new_second[None],
        grad_attention,
        new_anchors,
        new_momenta,
        merged.reshape(1, -1),
    )


def solution(mesh):
    return jax.shard_map(
        on_device,
        mesh=mesh,
        in_specs=(
            P(("rep", "node"), None),
            P(("rep", "node"), None),
            P(("rep", "node")),
            P("rep", "node", None),
            P("rep", "node", None),
            P("rep", "node", None),
            P("rep", None),
            P(),
            P("rep", "node", None),
            P(None, "node"),
            P(None, "node"),
            P("rep", "node"),
        ),
        out_specs=(
            P("rep", "node", None),
            P("rep", "node", None),
            P("rep", "node", None),
            P(("rep", "node"), None),
            P(None, "node"),
            P(None, "node"),
            P("rep", None),
        ),
        check_vma=False,
    )
```
